512 devices in a mesh: nodes: 512 (over z, x, y, core).
Axes of the slice: x: 4, y: 4, z: 16, core: 2. Of those that a mesh axis runs over, the one named last changes fastest.
Arguments:
- tangent: float32 [2, 393216, 128], P(None, 'nodes'), as said below
- base_v: float32 [4, 393216], P(None, 'nodes'), may hold values from -2 to 2
- coupling: bfloat16 [1536, 8, 256, 256], P('nodes'), may hold values from -0.125 to 0.125
- columns: int32 [1536, 8], P('nodes'), may hold values from 0 to 1535, as said below
Outputs:
- basis: float32 [2, 393216, 128], P(None, 'nodes')
- growth: float32 [128, 128], replicated
The draws below stay inside these ranges and needn't reach their ends.
Inputs may be any that keep to these rules, and one draw needn't show every extreme that they name: Block row r, held by index d = r // 3 of nodes, names 8 different block columns, all held by indices d - 1, d or d + 1 (cyclic over the axis). `tangent`: finite values.
All inputs are finite; a program needn't handle non-finite values.
Results may differ from the reference program's by a relative error of at most 0.00046.
Values may be sent and summed in bfloat16 or wider, within the bound.
A program may use at most 64 MiB of HBM per device.

```python
import math
import jax
import jax.numpy as jnp
from jax import lax

BS = 256
LINKS = 8
K = 128
STEPS = 4
BLK_DEV = 3
BLOCKS = 1536
NODES = 393216


def draw_tangent(key, part):
    keys = jax.random.split(key, 3)
    row_scale = jnp.exp(jax.random.uniform(keys[1], (2, NODES, 1), jnp.float32) * math.log(10.0))
    col_scale = jnp.exp(jax.random.uniform(keys[2], (1, 1, K), jnp.float32) * math.log(4.0))
    values = jax.random.normal(keys[0], (2, NODES, K), jnp.float32)
    return values * row_scale * col_scale


def draw_columns(key, part):
    keys = jax.random.split(key, BLOCKS)
    perms = jax.vmap(lambda one: jax.random.permutation(one, 3 * BLK_DEV))(keys)[:, :LINKS]
    device = (jnp.arange(BLOCKS, dtype=jnp.int32) // BLK_DEV)[:, None]
    return (((device - 1) * BLK_DEV + perms.astype(jnp.int32)) % BLOCKS).astype(jnp.int32)


def steps_of(own_key, dims, cuts, low, largest):
    factor_of = 1.0
    for axis_at, blocks in cuts:
        steps = jax.random.uniform(jax.random.fold_in(jax.random.fold_in(own_key, 6), axis_at), (blocks,), jnp.float32, low / len(cuts), largest / len(cuts))
        factor_of = factor_of * jnp.repeat(jnp.exp(steps), dims[axis_at] // blocks).reshape((-1,) + (1,) * (len(dims) - 1 - axis_at))
    return factor_of


def centred(stream_key, dims, scale, bound, pieces=(), kind=jnp.bfloat16):
    entries = jax.random.normal(stream_key, dims, jnp.float32) * scale
    if len(pieces) > 0:
        entries = steps_of(stream_key, dims, pieces, -0.22, 0.18) * entries
    return jnp.clip(entries, min=-bound, max=bound).astype(kind)


def setup_inputs(seed: int = 0) -> dict:
    seeds = jax.random.split(jax.random.key(seed), 5)
    return {
        "tangent": draw_tangent(jax.random.fold_in(seeds[4], 71), 0),
        "base_v": jnp.clip(jax.random.uniform(seeds[1], (STEPS, NODES), jnp.float32, -2.0, 2.0) * steps_of(seeds[1], (STEPS, NODES), ((1, 512),), -0.4, 0.0), -2.0, 2.0),
        "coupling": centred(seeds[2], (BLOCKS, LINKS, BS, BS), (LINKS * BS) ** -0.5, 0.125, ((0, 512),)),
        "columns": draw_columns(jax.random.fold_in(seeds[4], 71), 0),
    }


time_step = 0.1
recovery_rate = 0.08
recovery_damp = 0.8

def block_rows(pair, rounded):
    weights, picks = pair
    chosen = rounded[picks]
    return jnp.einsum('kij,kjc->ic', weights.astype(jnp.float32), chosen.astype(jnp.float32))

def reference(tangent, base_v, coupling, columns):
    volt_rows = tangent[0]
    recov_rows = tangent[1]
    for section in range(STEPS):
        rounded = volt_rows.astype(jnp.bfloat16).reshape(BLOCKS, BS, K)
        coupled = lax.map(lambda pair: block_rows(pair, rounded), (coupling, columns)).reshape(NODES, K)
        volt = base_v[section][:, None]
        new_volt = volt_rows + time_step * ((1.0 - volt * volt) * volt_rows - recov_rows + coupled)
        new_recov = recov_rows + time_step * recovery_rate * (volt_rows - recovery_damp * recov_rows)
        volt_rows, recov_rows = (new_volt, new_recov)
    high = lax.Precision.HIGHEST
    gram = jnp.dot(volt_rows.T, volt_rows, precision=high) + jnp.dot(recov_rows.T, recov_rows, precision=high)
    lower = jnp.linalg.cholesky(gram)
    inverse = lax.linalg.triangular_solve(lower, jnp.eye(K, dtype=gram.dtype), left_side=True, lower=True)
    scale = jnp.sqrt(2.0 * NODES)
    basis = jnp.stack([jnp.dot(volt_rows, inverse.T, precision=high), jnp.dot(recov_rows, inverse.T, precision=high)]) * scale
    growth = lower.T / scale
    return (basis, growth)
```

```python
import functools

import jax
import jax.numpy as jnp
from jax import lax
from jax.experimental import pallas as pl
from jax.experimental.pallas import tpu as pltpu
from jax.sharding import PartitionSpec as P

STEPS = 4
MESH = pl.DeviceIdType.MESH
HIGH = lax.Precision.HIGHEST

time_step = 0.1
recovery_rate = 0.08
recovery_damp = 0.8


def tangent_kernel(
    devices, plane, tan_ref, v_ref, coup_ref, col_ref, state_ref, gram_ref,
    tv, tw, acc, coef, raw, weights, own, before, after, parts, got, zbuf, total,
    load_sem, send_sem, recv_sem, red_send, red_recv, out_sem,
):
    blocks, links, size, _ = coup_ref.shape
    rows, vectors = tv.shape
    count = 3 * blocks
    tall = devices // plane
    piece = vectors // plane
    me = lax.axis_index("nodes")
    level, place = me // plane, me % plane
    right, left = (me + 1) % devices, (me + devices - 1) % devices

    def plane_peer(k):
        return level * plane + (place + k) % plane

    def tall_peer(k):
        return ((level + k) % tall) * plane + place

    barrier = pltpu.get_barrier_semaphore()

    def greet(device):
        pl.semaphore_signal(barrier, inc=1, device_id=(device,), device_id_type=MESH)

    greet(left)
    greet(right)

    @pl.loop(1, plane)
    def _(k):
        greet(plane_peer(k))

    @pl.loop(1, tall)
    def _(k):
        greet(tall_peer(k))

    load = pltpu.make_async_copy(coup_ref, raw.at[pl.ds(0, blocks)], load_sem)
    load.start()
    raw[blocks, 0] = jnp.zeros((size, size), jnp.bfloat16)
    for b in range(blocks):
        span = pl.ds(b * size, size)
        own[0, span, :] = tan_ref[0, span, :].astype(jnp.bfloat16)
    pl.semaphore_wait(barrier, 2 + (plane - 1) + (tall - 1))

    def sends(step, b):
        span = pl.ds(b * size, size)
        return [
            pltpu.make_async_remote_copy(
                src_ref=own.at[step, span, :],
                dst_ref=dst.at[step, span, :],
                send_sem=send_sem.at[step, side, b],
                recv_sem=recv_sem.at[step, side, b],
                device_id=(target,),
                device_id_type=MESH,
            )
            for side, (dst, target) in enumerate(((before, right), (after, left)))
        ]

    for b in range(blocks):
        for copy in sends(0, b):
            copy.start()

    first = me * blocks
    names = [[(col_ref[r, k] - first + blocks * (devices + 1)) % (blocks * devices) for k in range(links)] for r in range(blocks)]
    volt = v_ref[...]
    factor = 1.0 + time_step * (1.0 - volt * volt)
    factor = jnp.concatenate([factor, factor], axis=0).T
    for s in range(STEPS):
        coef[s] = jnp.broadcast_to(factor[:, s : s + 1], (rows, vectors))
    load.wait()
    for r in range(blocks):
        for c in range(count):
            at_r, at_k = blocks, 0
            for k in range(links):
                hit = names[r][k] == c
                at_r = jnp.where(hit, r, at_r)
                at_k = jnp.where(hit, k, at_k)
            weights[pl.ds(r * size, size), pl.ds(c * size, size)] = raw[at_r, at_k]

    def product(row_span, c, value):
        return jnp.dot(
            weights[row_span, pl.ds(c * size, size)], value, preferred_element_type=jnp.float32
        )

    everything = pl.ds(0, rows)
    gram_w = None
    for s in range(STEPS):
        old_v = tan_ref[0] if s == 0 else tv[...]
        old_w = tan_ref[1] if s == 0 else tw[...]
        acc[...] = old_v * coef[s] - time_step * old_w
        tw[...] = old_w + time_step * recovery_rate * (old_v - recovery_damp * old_w)
        acc[...] += time_step * jnp.dot(
            weights[:, pl.ds(blocks * size, blocks * size)], own[s], preferred_element_type=jnp.float32
        )
        if s == STEPS - 1:
            last_w = tw[...]
            gram_w = lax.dot_general(
                last_w, last_w, (((0,), (0,)), ((), ())), precision=HIGH, preferred_element_type=jnp.float32
            )
            store_w = pltpu.make_async_copy(tw, state_ref.at[1], out_sem.at[1])
            store_w.start()
        for b in range(blocks):
            arrived = sends(s, b)
            span = pl.ds(b * size, size)
            arrived[0].wait_recv()
            arrived[1].wait_recv()
            if b < blocks - 1:
                acc[...] += time_step * (
                    product(everything, b, before[s, span, :])
                    + product(everything, 2 * blocks + b, after[s, span, :])
                )
        last = pl.ds((blocks - 1) * size, size)
        for r in range(blocks):
            span = pl.ds(r * size, size)
            new = acc[span, :] + time_step * (
                product(span, blocks - 1, before[s, last, :]) + product(span, count - 1, after[s, last, :])
            )
            tv[span, :] = new
            if s < STEPS - 1:
                own[s + 1, span, :] = new.astype(jnp.bfloat16)
                for copy in sends(s + 1, r):
                    copy.start()

    store_v = pltpu.make_async_copy(tv, state_ref.at[0], out_sem.at[0])
    store_v.start()
    last_v = tv[...]
    local = gram_w + lax.dot_general(
        last_v, last_v, (((0,), (0,)), ((), ())), precision=HIGH, preferred_element_type=jnp.float32
    )
    for i in range(plane):
        parts[i] = local[i * piece : (i + 1) * piece, :]

    def spread(phase, src, dst, target):
        return pltpu.make_async_remote_copy(
            src_ref=src,
            dst_ref=dst,
            send_sem=red_send.at[phase],
            recv_sem=red_recv.at[phase],
            device_id=(target,),
            device_id_type=MESH,
        )

    def all_of(phase, ref, slots):
        span = ref.at[pl.ds(0, slots)]
        return spread(phase, span, span, right)

    @pl.loop(1, plane)
    def _(k):
        peer = (place + k) % plane
        spread(0, parts.at[peer], got.at[k - 1], plane_peer(k)).start()

    all_of(0, got, plane - 1).wait_recv()
    mine = parts[place] + jnp.sum(got[...], axis=0)
    zbuf[level] = mine

    @pl.loop(1, tall)
    def _(k):
        spread(1, zbuf.at[level], zbuf.at[level], tall_peer(k)).start()

    all_of(1, zbuf, tall - 1).wait_recv()
    total[place] = jnp.sum(zbuf[...], axis=0)

    @pl.loop(1, plane)
    def _(k):
        spread(2, total.at[place], total.at[place], plane_peer(k)).start()

    all_of(2, total, plane - 1).wait_recv()
    for i in range(plane):
        gram_ref[i * piece : (i + 1) * piece, :] = total[i]

    for s in range(STEPS):
        for b in range(blocks):
            for copy in sends(s, b):
                copy.wait_send()
    all_of(0, got, plane - 1).wait_send()
    all_of(1, zbuf, tall - 1).wait_send()
    all_of(2, total, plane - 1).wait_send()
    store_w.wait()
    store_v.wait()


def factor_rows(gram, width):
    lane = lax.broadcasted_iota(jnp.int32, (8, width), 1)
    sub = lax.broadcasted_iota(jnp.int32, (8, width), 0)
    wide = lambda x: jnp.broadcast_to(x, (8, width))
    panels = [gram[8 * q : 8 * q + 8, :] for q in range(width // 8)]
    upper, inverse = [], []
    for p in range(width // 8):
        panel = panels[p]
        base = 8 * p
        cols = [wide(panel[:, base + k : base + k + 1]) for k in range(8)]
        diag = {(s, k): wide(cols[k][s : s + 1, :]) for k in range(8) for s in range(k, 8)}
        in_block = (lane >= base) & (lane < base + 8)
        mixed = jnp.where(in_block, jnp.where(lane - base == sub, 1.0, 0.0), panel)
        row_a = [wide(panel[s : s + 1, :]) for s in range(8)]
        row_c = [wide(mixed[s : s + 1, :]) for s in range(8)]
        inv = []
        for i in range(8):
            inv.append(lax.rsqrt(diag[i, i]))
            row_a[i] = row_a[i] * inv[i]
            row_c[i] = row_c[i] * inv[i]
            for s in range(i + 1, 8):
                diag[s, i] = diag[s, i] * inv[i]
            for s in range(i + 1, 8):
                for k in range(i + 1, s + 1):
                    diag[s, k] = diag[s, k] - diag[s, i] * diag[k, i]
                row_a[s] = row_a[s] - diag[s, i] * row_a[i]
                row_c[s] = row_c[s] - diag[s, i] * row_c[i]
        out_a, out_c = row_a[7], row_c[7]
        for s in range(7):
            out_a = jnp.where(sub == s, row_a[s], out_a)
            out_c = jnp.where(sub == s, row_c[s], out_c)
        upper.append(jnp.where(lane >= base + sub, out_a, 0.0))
        inverse.append(jnp.where(lane <= base + sub, out_c, 0.0))
        back = [None] * 8
        for i in range(7, -1, -1):
            value = row_c[i]
            for s in range(i + 1, 8):
                value = value - diag[s, i] * back[s]
            back[i] = value * inv[i]
        for q in range(p + 1, width // 8):
            value = jnp.where(in_block, 0.0, panels[q])
            for k in range(8):
                value = value - wide(panels[q][:, base + k : base + k + 1]) * back[k]
            panels[q] = value
    return upper, inverse


def basis_kernel(scale, gram_ref, state_ref, basis_ref, growth_ref, state, inverse, out, in_sem, out_sem):
    vectors = gram_ref.shape[0]
    load = pltpu.make_async_copy(state_ref, state, in_sem)
    load.start()
    upper, low = factor_rows(gram_ref[...], vectors)
    for p, (a, c) in enumerate(zip(upper, low)):
        growth_ref[8 * p : 8 * p + 8, :] = a * (1.0 / scale)
        inverse[8 * p : 8 * p + 8, :] = c * scale
    load.wait()
    for half in range(2):
        out[half] = lax.dot_general(
            state[half], inverse[...], (((1,), (1,)), ((), ())), precision=HIGH, preferred_element_type=jnp.float32
        )
        pltpu.make_async_copy(out.at[half], basis_ref.at[half], out_sem.at[half]).start()
    for half in range(2):
        pltpu.make_async_copy(out.at[half], basis_ref.at[half], out_sem.at[half]).wait()


def local(tangent, base_v, coupling, columns, *, plane=32):
    blocks, links, size, _ = coupling.shape
    _, rows, vectors = tangent.shape
    devices = lax.axis_size("nodes")
    count = 3 * blocks
    tall, piece = devices // plane, vectors // plane
    vmem = pl.BlockSpec(memory_space=pltpu.VMEM)
    anywhere = pl.BlockSpec(memory_space=pl.ANY)
    f32, bf16 = jnp.float32, jnp.bfloat16
    dma = pltpu.SemaphoreType.DMA
    state, gram = pl.pallas_call(
        functools.partial(tangent_kernel, devices, plane),
        out_shape=(
            jax.ShapeDtypeStruct((2, rows, vectors), f32),
            jax.ShapeDtypeStruct((vectors, vectors), f32),
        ),
        in_specs=[vmem, vmem, anywhere, pl.BlockSpec(memory_space=pltpu.SMEM)],
        out_specs=(anywhere, vmem),
        scratch_shapes=[
            pltpu.VMEM((rows, vectors), f32),
            pltpu.VMEM((rows, vectors), f32),
            pltpu.VMEM((rows, vectors), f32),
            pltpu.VMEM((STEPS, rows, vectors), f32),
            pltpu.VMEM((blocks + 1, links, size, size), bf16),
            pltpu.VMEM((rows, count * size), bf16),
            pltpu.VMEM((STEPS, rows, vectors), bf16),
            pltpu.VMEM((STEPS, rows, vectors), bf16),
            pltpu.VMEM((STEPS, rows, vectors), bf16),
            pltpu.VMEM((plane, piece, vectors), f32),
            pltpu.VMEM((plane - 1, piece, vectors), f32),
            pltpu.VMEM((tall, piece, vectors), f32),
            pltpu.VMEM((plane, piece, vectors), f32),
            dma,
            dma((STEPS, 2, blocks)),
            dma((STEPS, 2, blocks)),
            dma((3,)),
            dma((3,)),
            dma((2,)),
        ],
        compiler_params=pltpu.CompilerParams(
            collective_id=0, has_side_effects=True, vmem_limit_bytes=40 * 2**20
        ),
    )(tangent, base_v, coupling, columns)
    scale = float((2.0 * rows * devices) ** 0.5)
    return pl.pallas_call(
        functools.partial(basis_kernel, scale),
        out_shape=(
            jax.ShapeDtypeStruct((2, rows, vectors), f32),
            jax.ShapeDtypeStruct((vectors, vectors), f32),
        ),
        in_specs=[vmem, anywhere],
        out_specs=(anywhere, vmem),
        scratch_shapes=[
            pltpu.VMEM((2, rows, vectors), f32),
            pltpu.VMEM((vectors, vectors), f32),
            pltpu.VMEM((2, rows, vectors), f32),
            dma,
            dma((2,)),
        ],
        compiler_params=pltpu.CompilerParams(vmem_limit_bytes=40 * 2**20),
    )(gram, state)


def solution(mesh):
    placed = (
        P(None, "nodes", None),
        P(None, "nodes"),
        P("nodes", None, None, None),
        P("nodes", None),
    )
    return jax.shard_map(
        local, mesh=mesh, in_specs=placed, out_specs=(P(None, "nodes", None), P()), check_vma=False
    )
```

```python
import functools

import jax
import jax.numpy as jnp
from jax import lax
from jax.experimental import pallas as pl
from jax.experimental.pallas import tpu as pltpu
from jax.sharding import PartitionSpec as P

STEPS = 4
MESH = pl.DeviceIdType.MESH
HIGH = lax.Precision.HIGHEST

time_step = 0.1
recovery_rate = 0.08
recovery_damp = 0.8


def tangent_kernel(
    devices, grid, tan_ref, v_hbm, coup_ref, col_hbm, state_ref, gram_ref,
    v_ref, col_ref, tv, tw, acc, coef, raw, weights, own, before, after, parts, got, zbuf, total,
    load_sem, send_sem, recv_sem, red_send, red_recv, out_sem,
):
    blocks, links, size, _ = coup_ref.shape
    rows, vectors = tv.shape
    count = 3 * blocks
    plane = grid[0] * grid[1] * grid[2]
    tall = devices // plane
    piece = vectors // plane
    me = lax.axis_index("nodes")
    level, place = me // plane, me % plane
    right, left = (me + 1) % devices, (me + devices - 1) % devices

    around = lambda shift, size: min(shift, size - shift)
    shifts = sorted(
        ((a, b, c) for a in range(grid[0]) for b in range(grid[1]) for c in range(grid[2]) if a + b + c > 0),
        key=lambda t: -(4 * around(t[0], grid[0]) + 4 * around(t[1], grid[1]) + t[2]),
    )
    at_a, at_b, at_c = place // (grid[1] * grid[2]), place // grid[2] % grid[1], place % grid[2]
    plane_peers = [
        ((at_a + a) % grid[0] * grid[1] + (at_b + b) % grid[1]) * grid[2] + (at_c + c) % grid[2]
        for a, b, c in shifts
    ]
    tall_peers = [
        (level + k) % tall * plane + place for k in sorted(range(1, tall), key=lambda k: -around(k, tall))
    ]

    loads = [
        pltpu.make_async_copy(src, dst, load_sem.at[i])
        for i, (src, dst) in enumerate(
            (
                (tan_ref.at[0], tv),
                (col_hbm, col_ref),
                (v_hbm, v_ref),
                (coup_ref, raw.at[pl.ds(0, blocks)]),
                (tan_ref.at[1], tw),
            )
        )
    ]
    loads[0].start()
    barrier = pltpu.get_barrier_semaphore()

    def greet(device):
        pl.semaphore_signal(barrier, inc=1, device_id=(device,), device_id_type=MESH)

    for peer in tall_peers:
        greet(peer)
    for peer in plane_peers:
        greet(level * plane + peer)
    greet(left)
    greet(right)
    for load in loads[1:]:
        load.start()
    raw[blocks, 0] = jnp.zeros((size, size), jnp.bfloat16)
    loads[0].wait()
    for b in range(blocks):
        span = pl.ds(b * size, size)
        own[0, span, :] = tv[span, :].astype(jnp.bfloat16)
    pl.semaphore_wait(barrier, 2 + (plane - 1) + (tall - 1))

    def sends(step, b):
        span = pl.ds(b * size, size)
        return [
            pltpu.make_async_remote_copy(
                src_ref=own.at[step, span, :],
                dst_ref=dst.at[step, span, :],
                send_sem=send_sem.at[step, side, b],
                recv_sem=recv_sem.at[step, side, b],
                device_id=(target,),
                device_id_type=MESH,
            )
            for side, (dst, target) in enumerate(((before, right), (after, left)))
        ]

    for b in range(blocks):
        for copy in sends(0, b):
            copy.start()

    loads[1].wait()
    first = me * blocks
    names = [[(col_ref[r, k] - first + blocks * (devices + 1)) % (blocks * devices) for k in range(links)] for r in range(blocks)]
    loads[2].wait()
    volt = v_ref[...]
    factor = 1.0 + time_step * (1.0 - volt * volt)
    factor = jnp.concatenate([factor, factor], axis=0).T
    for s in range(STEPS):
        coef[s] = jnp.broadcast_to(factor[:, s : s + 1], (rows, vectors))
    loads[3].wait()
    for r in range(blocks):
        for c in range(count):
            at_r, at_k = blocks, 0
            for k in range(links):
                hit = names[r][k] == c
                at_r = jnp.where(hit, r, at_r)
                at_k = jnp.where(hit, k, at_k)
            weights[pl.ds(r * size, size), pl.ds(c * size, size)] = raw[at_r, at_k]

    def product(row_span, c, value):
        return jnp.dot(
            weights[row_span, pl.ds(c * size, size)], value, preferred_element_type=jnp.float32
        )

    loads[4].wait()
    everything = pl.ds(0, rows)
    gram_w = None
    for s in range(STEPS):
        old_v, old_w = tv[...], tw[...]
        acc[...] = old_v * coef[s] - time_step * old_w
        tw[...] = old_w + time_step * recovery_rate * (old_v - recovery_damp * old_w)
        acc[...] += time_step * jnp.dot(
            weights[:, pl.ds(blocks * size, blocks * size)], own[s], preferred_element_type=jnp.float32
        )
        if s == STEPS - 1:
            last_w = tw[...]
            gram_w = lax.dot_general(
                last_w, last_w, (((0,), (0,)), ((), ())), precision=HIGH, preferred_element_type=jnp.float32
            )
            store_w = pltpu.make_async_copy(tw, state_ref.at[1], out_sem.at[1])
            store_w.start()
        for b in range(blocks):
            arrived = sends(s, b)
            span = pl.ds(b * size, size)
            arrived[0].wait_recv()
            arrived[1].wait_recv()
            if b < blocks - 1:
                acc[...] += time_step * (
                    product(everything, b, before[s, span, :])
                    + product(everything, 2 * blocks + b, after[s, span, :])
                )
        last = pl.ds((blocks - 1) * size, size)
        for r in range(blocks):
            span = pl.ds(r * size, size)
            new = acc[span, :] + time_step * (
                product(span, blocks - 1, before[s, last, :]) + product(span, count - 1, after[s, last, :])
            )
            tv[span, :] = new
            if s < STEPS - 1:
                own[s + 1, span, :] = new.astype(jnp.bfloat16)
                for copy in sends(s + 1, r):
                    copy.start()

    store_v = pltpu.make_async_copy(tv, state_ref.at[0], out_sem.at[0])
    store_v.start()
    last_v = tv[...]
    local = gram_w + lax.dot_general(
        last_v, last_v, (((0,), (0,)), ((), ())), precision=HIGH, preferred_element_type=jnp.float32
    )
    for i in range(plane):
        parts[i] = local[i * piece : (i + 1) * piece, :]

    def spread(phase, src, dst, target):
        return pltpu.make_async_remote_copy(
            src_ref=src,
            dst_ref=dst,
            send_sem=red_send.at[phase],
            recv_sem=red_recv.at[phase],
            device_id=(target,),
            device_id_type=MESH,
        )

    def all_of(phase, ref, slots):
        span = ref.at[pl.ds(0, slots)]
        return spread(phase, span, span, right)

    for k, peer in enumerate(plane_peers):
        spread(0, parts.at[peer], got.at[k], level * plane + peer).start()

    all_of(0, got, plane - 1).wait_recv()
    mine = parts[place] + jnp.sum(got[...], axis=0)
    zbuf[level] = mine

    for peer in tall_peers:
        spread(1, zbuf.at[level], zbuf.at[level], peer).start()

    all_of(1, zbuf, tall - 1).wait_recv()
    total[place] = jnp.sum(zbuf[...], axis=0)

    for peer in plane_peers:
        spread(2, total.at[place], total.at[place], level * plane + peer).start()

    all_of(2, total, plane - 1).wait_recv()
    for i in range(plane):
        gram_ref[i * piece : (i + 1) * piece, :] = total[i]

    for s in range(STEPS):
        for b in range(blocks):
            for copy in sends(s, b):
                copy.wait_send()
    all_of(0, got, plane - 1).wait_send()
    all_of(1, zbuf, tall - 1).wait_send()
    all_of(2, total, plane - 1).wait_send()
    store_w.wait()
    store_v.wait()


def factor_rows(gram, width):
    lane = lax.broadcasted_iota(jnp.int32, (8, width), 1)
    sub = lax.broadcasted_iota(jnp.int32, (8, width), 0)
    wide = lambda x: jnp.broadcast_to(x, (8, width))
    count = width // 8
    panels = [gram[8 * q : 8 * q + 8, :] for q in range(count)]
    upper, inverse = [], []
    for p in range(count):
        panel = panels[p]
        base = 8 * p
        cols = [wide(panel[:, base + k : base + k + 1]) for k in range(8)]
        diag = {(s, k): wide(cols[k][s : s + 1, :]) for k in range(8) for s in range(k, 8)}
        in_block = (lane >= base) & (lane < base + 8)
        mixed = jnp.where(in_block, jnp.where(lane - base == sub, 1.0, 0.0), panel)
        row_a = [wide(panel[s : s + 1, :]) for s in range(8)]
        row_c = [wide(mixed[s : s + 1, :]) for s in range(8)]
        nxt = [wide(panels[p + 1][:, base + k : base + k + 1]) for k in range(8)] if p + 1 < count else None
        nval = jnp.where(in_block, 0.0, panels[p + 1]) if p + 1 < count else None
        inv = []
        for i in range(8):
            inv.append(lax.rsqrt(diag[i, i]))
            row_a[i] = row_a[i] * inv[i]
            row_c[i] = row_c[i] * inv[i]
            if nxt: nxt[i] = nxt[i] * inv[i]
            for s in range(i + 1, 8):
                diag[s, i] = diag[s, i] * inv[i]
            for s in range(i + 1, 8):
                for k in range(i + 1, s + 1):
                    diag[s, k] = diag[s, k] - diag[s, i] * diag[k, i]
                row_a[s] = row_a[s] - diag[s, i] * row_a[i]
                row_c[s] = row_c[s] - diag[s, i] * row_c[i]
                if nxt: nxt[s] = nxt[s] - diag[s, i] * nxt[i]
            if nxt: nval = nval - nxt[i] * row_c[i]
        out_a, out_c = row_a[7], row_c[7]
        for s in range(7):
            out_a = jnp.where(sub == s, row_a[s], out_a)
            out_c = jnp.where(sub == s, row_c[s], out_c)
        upper.append(jnp.where(lane >= base + sub, out_a, 0.0))
        inverse.append(jnp.where(lane <= base + sub, out_c, 0.0))
        if nxt:
            panels[p + 1] = nval
        back = [None] * 8
        for i in range(7, -1, -1):
            value = row_c[i]
            for s in range(i + 1, 8):
                value = value - diag[s, i] * back[s]
            back[i] = value * inv[i]
        for q in range(p + 2, count):
            value = jnp.where(in_block, 0.0, panels[q])
            for k in range(8):
                value = value - wide(panels[q][:, base + k : base + k + 1]) * back[k]
            panels[q] = value
    return upper, inverse


def basis_kernel(scale, gram_ref, state_ref, basis_ref, growth_ref, state, inverse, out, in_sem, out_sem):
    vectors = gram_ref.shape[0]
    load = pltpu.make_async_copy(state_ref, state, in_sem)
    load.start()
    upper, low = factor_rows(gram_ref[...], vectors)
    for p, (a, c) in enumerate(zip(upper, low)):
        growth_ref[8 * p : 8 * p + 8, :] = a * (1.0 / scale)
        inverse[8 * p : 8 * p + 8, :] = c * scale
    load.wait()
    for half in range(2):
        out[half] = lax.dot_general(
            state[half], inverse[...], (((1,), (1,)), ((), ())), precision=HIGH, preferred_element_type=jnp.float32
        )
        pltpu.make_async_copy(out.at[half], basis_ref.at[half], out_sem.at[half]).start()
    for half in range(2):
        pltpu.make_async_copy(out.at[half], basis_ref.at[half], out_sem.at[half]).wait()


def local(tangent, base_v, coupling, columns, *, grid=(4, 4, 2)):
    blocks, links, size, _ = coupling.shape
    _, rows, vectors = tangent.shape
    devices = lax.axis_size("nodes")
    count = 3 * blocks
    plane = grid[0] * grid[1] * grid[2]
    tall, piece = devices // plane, vectors // plane
    vmem = pl.BlockSpec(memory_space=pltpu.VMEM)
    anywhere = pl.BlockSpec(memory_space=pl.ANY)
    f32, bf16 = jnp.float32, jnp.bfloat16
    dma = pltpu.SemaphoreType.DMA
    state, gram = pl.pallas_call(
        functools.partial(tangent_kernel, devices, grid),
        out_shape=(
            jax.ShapeDtypeStruct((2, rows, vectors), f32),
            jax.ShapeDtypeStruct((vectors, vectors), f32),
        ),
        in_specs=[pl.BlockSpec(memory_space=pltpu.HBM)] * 4,
        out_specs=(anywhere, vmem),
        scratch_shapes=[
            pltpu.VMEM((STEPS, rows), f32),
            pltpu.SMEM((blocks, links), jnp.int32),
            pltpu.VMEM((rows, vectors), f32),
            pltpu.VMEM((rows, vectors), f32),
            pltpu.VMEM((rows, vectors), f32),
            pltpu.VMEM((STEPS, rows, vectors), f32),
            pltpu.VMEM((blocks + 1, links, size, size), bf16),
            pltpu.VMEM((rows, count * size), bf16),
            pltpu.VMEM((STEPS, rows, vectors), bf16),
            pltpu.VMEM((STEPS, rows, vectors), bf16),
            pltpu.VMEM((STEPS, rows, vectors), bf16),
            pltpu.VMEM((plane, piece, vectors), f32),
            pltpu.VMEM((plane - 1, piece, vectors), f32),
            pltpu.VMEM((tall, piece, vectors), f32),
            pltpu.VMEM((plane, piece, vectors), f32),
            dma((5,)),
            dma((STEPS, 2, blocks)),
            dma((STEPS, 2, blocks)),
            dma((3,)),
            dma((3,)),
            dma((2,)),
        ],
        compiler_params=pltpu.CompilerParams(
            collective_id=0, has_side_effects=True, vmem_limit_bytes=40 * 2**20
        ),
    )(*(pltpu.with_memory_space_constraint(x, pltpu.HBM) for x in (tangent, base_v, coupling, columns)))
    scale = float((2.0 * rows * devices) ** 0.5)
    return pl.pallas_call(
        functools.partial(basis_kernel, scale),
        out_shape=(
            jax.ShapeDtypeStruct((2, rows, vectors), f32),
            jax.ShapeDtypeStruct((vectors, vectors), f32),
        ),
        in_specs=[vmem, anywhere],
        out_specs=(anywhere, vmem),
        scratch_shapes=[
            pltpu.VMEM((2, rows, vectors), f32),
            pltpu.VMEM((vectors, vectors), f32),
            pltpu.VMEM((2, rows, vectors), f32),
            dma,
            dma((2,)),
        ],
        compiler_params=pltpu.CompilerParams(vmem_limit_bytes=40 * 2**20),
    )(gram, state)


def solution(mesh):
    placed = (
        P(None, "nodes", None),
        P(None, "nodes"),
        P("nodes", None, None, None),
        P("nodes", None),
    )
    return jax.shard_map(
        local, mesh=mesh, in_specs=placed, out_specs=(P(None, "nodes", None), P()), check_vma=False
    )
```

```python
import functools

import jax
import jax.numpy as jnp
from jax import lax
from jax.experimental import pallas as pl
from jax.experimental.pallas import tpu as pltpu
from jax.sharding import PartitionSpec as P

STEPS = 4
GROUPS = 2
MESH = pl.DeviceIdType.MESH
HIGH = lax.Precision.HIGHEST

time_step = 0.1
recovery_rate = 0.08
recovery_damp = 0.8


def tangent_kernel(
    devices, grid, tan_ref, v_hbm, coup_ref, col_hbm, state_ref, gram_ref,
    v_ref, col_ref, full, sv, sw, acc, coef, raw, weights, own, near, far, parts, got, zbuf, total,
    load_sem, send_sem, recv_sem, red_send, red_recv, out_sem,
):
    blocks, links, size, _ = coup_ref.shape
    _, rows, vectors = full.shape
    half, lanes = size // 2, vectors // 2
    packed = rows // 2
    count = 3 * blocks
    plane = grid[0] * grid[1] * grid[2]
    tall = devices // plane
    piece = vectors // plane
    me = lax.axis_index("nodes")
    level, place = me // plane, me % plane
    odd = me % 2
    partner = me + 1 - 2 * odd
    other = (me + devices - 1 + 2 * odd) % devices

    around = lambda shift, size: min(shift, size - shift)
    shifts = sorted(
        ((a, b, c) for a in range(grid[0]) for b in range(grid[1]) for c in range(grid[2]) if a + b + c > 0),
        key=lambda t: -(4 * around(t[0], grid[0]) + 4 * around(t[1], grid[1]) + t[2]),
    )
    at_a, at_b, at_c = place // (grid[1] * grid[2]), place // grid[2] % grid[1], place % grid[2]
    plane_peers = [
        ((at_a + a) % grid[0] * grid[1] + (at_b + b) % grid[1]) * grid[2] + (at_c + c) % grid[2]
        for a, b, c in shifts
    ]
    tall_peers = [
        (level + k) % tall * plane + place for k in sorted(range(1, tall), key=lambda k: -around(k, tall))
    ]

    loads = [
        pltpu.make_async_copy(src, dst, load_sem.at[i])
        for i, (src, dst) in enumerate(
            (
                (tan_ref.at[0], full.at[0]),
                (col_hbm, col_ref),
                (v_hbm, v_ref),
                (coup_ref, raw.at[pl.ds(0, blocks)]),
                (tan_ref.at[1], full.at[1]),
            )
        )
    ]
    loads[0].start()
    barrier = pltpu.get_barrier_semaphore()

    def greet(device):
        pl.semaphore_signal(barrier, inc=1, device_id=(device,), device_id_type=MESH)

    for peer in tall_peers:
        greet(peer)
    for peer in plane_peers:
        greet(level * plane + peer)
    greet(other)
    greet(partner)
    for load in loads[1:]:
        load.start()
    raw[blocks, 0] = jnp.zeros((size, size), jnp.bfloat16)
    low = lax.broadcasted_iota(jnp.int32, (half, vectors), 1) < lanes

    def turn(x):
        return pltpu.roll(x, lanes, axis=1)

    def pack(which, store):
        for b in range(blocks):
            top = full[which, pl.ds(b * size, half), :]
            bottom = full[which, pl.ds(b * size + half, half), :]
            store(0, b, jnp.where(low, top, turn(bottom)))
            store(1, b, jnp.where(low, turn(top), bottom))

    def unpack(which, group):
        for b in range(blocks):
            zero, one = group[0, pl.ds(b * half, half), :], group[1, pl.ds(b * half, half), :]
            full[which, pl.ds(b * size, half), :] = jnp.where(low, zero, turn(one))
            full[which, pl.ds(b * size + half, half), :] = jnp.where(low, turn(zero), one)

    def start_voltage(g, b, value):
        sv[g, pl.ds(b * half, half), :] = value
        own[0, g, pl.ds(b * half, half), :] = value.astype(jnp.bfloat16)

    def start_recovery(g, b, value):
        sw[g, pl.ds(b * half, half), :] = value

    loads[0].wait()
    pack(0, start_voltage)
    pl.semaphore_wait(barrier, 2 + (plane - 1) + (tall - 1))

    def send(step, g, b, side):
        span = pl.ds(b * half, half)
        dst, target = ((near, partner), (far, other))[side]
        return pltpu.make_async_remote_copy(
            src_ref=own.at[step, g, span, :],
            dst_ref=dst.at[step, g, span, :],
            send_sem=send_sem.at[step, g, side, b],
            recv_sem=recv_sem.at[step, g, side, b],
            device_id=(target,),
            device_id_type=MESH,
        )

    for g in range(GROUPS):
        for b in range(blocks):
            send(0, g, b, 1).start()
            send(0, g, b, 0).start()

    loads[1].wait()
    first = me * blocks
    names = [[(col_ref[r, k] - first + blocks * (devices + 1)) % (blocks * devices) for k in range(links)] for r in range(blocks)]
    loads[2].wait()
    volt = v_ref[...]
    factor = 1.0 + time_step * (1.0 - volt * volt)
    factor = jnp.concatenate([factor, factor], axis=0).T
    for s in range(STEPS):
        for b in range(blocks):
            top, bottom = (
                jnp.broadcast_to(factor[b * size + at : b * size + at + half, s : s + 1], (half, vectors))
                for at in (0, half)
            )
            coef[s, pl.ds(b * half, half), :] = jnp.where(low, top, bottom)
    loads[3].wait()
    starts = (blocks, 2 * blocks * (1 - odd), 2 * blocks * odd)
    for r in range(blocks):
        for c in range(count):
            at_r, at_k = blocks, 0
            for k in range(links):
                hit = names[r][k] == starts[c // blocks] + c % blocks
                at_r = jnp.where(hit, r, at_r)
                at_k = jnp.where(hit, k, at_k)
            block = raw[at_r, at_k]
            weights[pl.ds(r * size, half), pl.ds(c * size, size)] = block[:half]
            for side in range(2):
                weights[pl.ds(r * size + half, half), pl.ds(c * size + side * half, half)] = block[
                    half:, (1 - side) * half : (2 - side) * half
                ]

    def both(*values):
        return jnp.concatenate([y for x in values for y in (x, turn(x))], axis=0)

    def product(row_span, at, operand):
        return jnp.dot(
            weights[row_span, pl.ds(at * size, operand.shape[0])], operand, preferred_element_type=jnp.float32
        )

    def own_part(s, g):
        old_v, old_w = sv[g], sw[g]
        sv[g] = old_v * coef[s] - time_step * old_w
        sw[g] = old_w + time_step * recovery_rate * (old_v - recovery_damp * old_w)
        operand = both(*(own[s, g, pl.ds(b * half, half), :] for b in range(blocks)))
        acc[g] = product(pl.ds(0, rows), 0, operand)

    def near_part(s, g):
        for b in range(blocks):
            send(s, g, b, 0).wait_recv()
        operand = both(*(near[s, g, pl.ds(b * half, half), :] for b in range(blocks)))
        acc[g] += product(pl.ds(0, rows), blocks, operand)

    def finish(s, g):
        for b in range(blocks):
            send(s, g, b, 1).wait_recv()
        operand = both(*(far[s, g, pl.ds(b * half, half), :] for b in range(blocks)))
        for r in range(blocks):
            span = pl.ds(r * half, half)
            here = pl.ds(r * size, size)
            coupled = acc[g, here, :] + product(here, 2 * blocks, operand)
            new = sv[g, span, :] + time_step * jnp.where(low, coupled[:half], coupled[half:])
            sv[g, span, :] = new
            if s < STEPS - 1:
                own[s + 1, g, span, :] = new.astype(jnp.bfloat16)
                send(s + 1, g, r, 1).start()
                send(s + 1, g, r, 0).start()

    def gram_of(which):
        x = full[which]
        return lax.dot_general(
            x, x, (((0,), (0,)), ((), ())), precision=HIGH, preferred_element_type=jnp.float32
        )

    loads[4].wait()
    pack(1, start_recovery)
    for g in range(GROUPS):
        own_part(0, g)
    for s in range(STEPS):
        for g in range(GROUPS):
            near_part(s, g)
        for g in range(GROUPS):
            finish(s, g)
            if s < STEPS - 1:
                own_part(s + 1, g)
        if s == STEPS - 2:
            unpack(1, sw)
            store_w = pltpu.make_async_copy(full.at[1], state_ref.at[1], out_sem.at[1])
            store_w.start()
            gram_w = gram_of(1)
    unpack(0, sv)
    store_v = pltpu.make_async_copy(full.at[0], state_ref.at[0], out_sem.at[0])
    store_v.start()
    local = gram_w + gram_of(0)
    for i in range(plane):
        parts[i] = local[i * piece : (i + 1) * piece, :]

    def spread(phase, src, dst, target):
        return pltpu.make_async_remote_copy(
            src_ref=src,
            dst_ref=dst,
            send_sem=red_send.at[phase],
            recv_sem=red_recv.at[phase],
            device_id=(target,),
            device_id_type=MESH,
        )

    def all_of(phase, ref, slots):
        span = ref.at[pl.ds(0, slots)]
        return spread(phase, span, span, partner)

    for k, peer in enumerate(plane_peers):
        spread(0, parts.at[peer], got.at[k], level * plane + peer).start()

    all_of(0, got, plane - 1).wait_recv()
    mine = parts[place] + jnp.sum(got[...], axis=0)
    zbuf[level] = mine

    for peer in tall_peers:
        spread(1, zbuf.at[level], zbuf.at[level], peer).start()

    all_of(1, zbuf, tall - 1).wait_recv()
    total[place] = jnp.sum(zbuf[...], axis=0)

    for peer in plane_peers:
        spread(2, total.at[place], total.at[place], level * plane + peer).start()

    all_of(2, total, plane - 1).wait_recv()
    for i in range(plane):
        gram_ref[i * piece : (i + 1) * piece, :] = total[i]

    for s in range(STEPS):
        for g in range(GROUPS):
            for b in range(blocks):
                for side in range(2):
                    send(s, g, b, side).wait_send()
    all_of(0, got, plane - 1).wait_send()
    all_of(1, zbuf, tall - 1).wait_send()
    all_of(2, total, plane - 1).wait_send()
    store_w.wait()
    store_v.wait()


def factor_rows(gram, width):
    lane = lax.broadcasted_iota(jnp.int32, (8, width), 1)
    sub = lax.broadcasted_iota(jnp.int32, (8, width), 0)
    wide = lambda x: jnp.broadcast_to(x, (8, width))
    count = width // 8
    panels = [gram[8 * q : 8 * q + 8, :] for q in range(count)]
    upper, inverse = [], []
    for p in range(count):
        panel = panels[p]
        base = 8 * p
        cols = [wide(panel[:, base + k : base + k + 1]) for k in range(8)]
        diag = {(s, k): wide(cols[k][s : s + 1, :]) for k in range(8) for s in range(k, 8)}
        in_block = (lane >= base) & (lane < base + 8)
        mixed = jnp.where(in_block, jnp.where(lane - base == sub, 1.0, 0.0), panel)
        row_a = [wide(panel[s : s + 1, :]) for s in range(8)]
        row_c = [wide(mixed[s : s + 1, :]) for s in range(8)]
        nxt = [wide(panels[p + 1][:, base + k : base + k + 1]) for k in range(8)] if p + 1 < count else None
        nval = jnp.where(in_block, 0.0, panels[p + 1]) if p + 1 < count else None
        inv = []
        for i in range(8):
            inv.append(lax.rsqrt(diag[i, i]))
            row_a[i] = row_a[i] * inv[i]
            row_c[i] = row_c[i] * inv[i]
            if nxt: nxt[i] = nxt[i] * inv[i]
            for s in range(i + 1, 8):
                diag[s, i] = diag[s, i] * inv[i]
            for s in range(i + 1, 8):
                for k in range(i + 1, s + 1):
                    diag[s, k] = diag[s, k] - diag[s, i] * diag[k, i]
                row_a[s] = row_a[s] - diag[s, i] * row_a[i]
                row_c[s] = row_c[s] - diag[s, i] * row_c[i]
                if nxt: nxt[s] = nxt[s] - diag[s, i] * nxt[i]
            if nxt: nval = nval - nxt[i] * row_c[i]
        out_a, out_c = row_a[7], row_c[7]
        for s in range(7):
            out_a = jnp.where(sub == s, row_a[s], out_a)
            out_c = jnp.where(sub == s, row_c[s], out_c)
        upper.append(jnp.where(lane >= base + sub, out_a, 0.0))
        inverse.append(jnp.where(lane <= base + sub, out_c, 0.0))
        if nxt:
            panels[p + 1] = nval
        back = [None] * 8
        for i in range(7, -1, -1):
            value = row_c[i]
            for s in range(i + 1, 8):
                value = value - diag[s, i] * back[s]
            back[i] = value * inv[i]
        for q in range(p + 2, count):
            value = jnp.where(in_block, 0.0, panels[q])
            for k in range(8):
                value = value - wide(panels[q][:, base + k : base + k + 1]) * back[k]
            panels[q] = value
    return upper, inverse


def basis_kernel(scale, gram_ref, state_ref, basis_ref, growth_ref, state, inverse, out, in_sem, out_sem):
    vectors = gram_ref.shape[0]
    load = pltpu.make_async_copy(state_ref, state, in_sem)
    load.start()
    upper, low = factor_rows(gram_ref[...], vectors)
    for p, (a, c) in enumerate(zip(upper, low)):
        growth_ref[8 * p : 8 * p + 8, :] = a * (1.0 / scale)
        inverse[8 * p : 8 * p + 8, :] = c * scale
    load.wait()
    for half in range(2):
        out[half] = lax.dot_general(
            state[half], inverse[...], (((1,), (1,)), ((), ())), precision=HIGH, preferred_element_type=jnp.float32
        )
        pltpu.make_async_copy(out.at[half], basis_ref.at[half], out_sem.at[half]).start()
    for half in range(2):
        pltpu.make_async_copy(out.at[half], basis_ref.at[half], out_sem.at[half]).wait()


def local(tangent, base_v, coupling, columns, *, grid=(4, 4, 2)):
    blocks, links, size, _ = coupling.shape
    _, rows, vectors = tangent.shape
    devices = lax.axis_size("nodes")
    count = 3 * blocks
    plane = grid[0] * grid[1] * grid[2]
    tall, piece = devices // plane, vectors // plane
    vmem = pl.BlockSpec(memory_space=pltpu.VMEM)
    anywhere = pl.BlockSpec(memory_space=pl.ANY)
    f32, bf16 = jnp.float32, jnp.bfloat16
    dma = pltpu.SemaphoreType.DMA
    state, gram = pl.pallas_call(
        functools.partial(tangent_kernel, devices, grid),
        out_shape=(
            jax.ShapeDtypeStruct((2, rows, vectors), f32),
            jax.ShapeDtypeStruct((vectors, vectors), f32),
        ),
        in_specs=[pl.BlockSpec(memory_space=pltpu.HBM)] * 4,
        out_specs=(anywhere, vmem),
        scratch_shapes=[
            pltpu.VMEM((STEPS, rows), f32),
            pltpu.SMEM((blocks, links), jnp.int32),
            pltpu.VMEM((2, rows, vectors), f32),
            pltpu.VMEM((GROUPS, rows // 2, vectors), f32),
            pltpu.VMEM((GROUPS, rows // 2, vectors), f32),
            pltpu.VMEM((GROUPS, rows, vectors), f32),
            pltpu.VMEM((STEPS, rows // 2, vectors), f32),
            pltpu.VMEM((blocks + 1, links, size, size), bf16),
            pltpu.VMEM((rows, count * size), bf16),
            pltpu.VMEM((STEPS, GROUPS, rows // 2, vectors), bf16),
            pltpu.VMEM((STEPS, GROUPS, rows // 2, vectors), bf16),
            pltpu.VMEM((STEPS, GROUPS, rows // 2, vectors), bf16),
            pltpu.VMEM((plane, piece, vectors), f32),
            pltpu.VMEM((plane - 1, piece, vectors), f32),
            pltpu.VMEM((tall, piece, vectors), f32),
            pltpu.VMEM((plane, piece, vectors), f32),
            dma((5,)),
            dma((STEPS, GROUPS, 2, blocks)),
            dma((STEPS, GROUPS, 2, blocks)),
            dma((3,)),
            dma((3,)),
            dma((2,)),
        ],
        compiler_params=pltpu.CompilerParams(
            collective_id=0, has_side_effects=True, vmem_limit_bytes=40 * 2**20
        ),
    )(*(pltpu.with_memory_space_constraint(x, pltpu.HBM) for x in (tangent, base_v, coupling, columns)))
    scale = float((2.0 * rows * devices) ** 0.5)
    return pl.pallas_call(
        functools.partial(basis_kernel, scale),
        out_shape=(
            jax.ShapeDtypeStruct((2, rows, vectors), f32),
            jax.ShapeDtypeStruct((vectors, vectors), f32),
        ),
        in_specs=[vmem, anywhere],
        out_specs=(anywhere, vmem),
        scratch_shapes=[
            pltpu.VMEM((2, rows, vectors), f32),
            pltpu.VMEM((vectors, vectors), f32),
            pltpu.VMEM((2, rows, vectors), f32),
            dma,
            dma((2,)),
        ],
        compiler_params=pltpu.CompilerParams(vmem_limit_bytes=40 * 2**20),
    )(gram, state)


def solution(mesh):
    placed = (
        P(None, "nodes", None),
        P(None, "nodes"),
        P("nodes", None, None, None),
        P("nodes", None),
    )
    return jax.shard_map(
        local, mesh=mesh, in_specs=placed, out_specs=(P(None, "nodes", None), P()), check_vma=False
    )
```

```python
import functools

import jax
import jax.numpy as jnp
from jax import lax
from jax.experimental import pallas as pl
from jax.experimental.pallas import tpu as pltpu
from jax.sharding import PartitionSpec as P

STEPS = 4
GROUPS = 2
PIECES = 3
MESH = pl.DeviceIdType.MESH
HIGH = lax.Precision.HIGHEST

time_step = 0.1
recovery_rate = 0.08
recovery_damp = 0.8


def tangent_kernel(
    devices, grid, tan_ref, v_hbm, coup_ref, col_hbm, state_ref, gram_ref,
    v_ref, col_ref, full, sv, sw, acc, coef, raw, weights, own, near, far, parts, got, zbuf, total,
    load_sem, send_sem, recv_sem, red_send, red_recv, out_sem,
):
    blocks, links, size, _ = coup_ref.shape
    _, rows, vectors = full.shape
    half, lanes = size // 2, vectors // 2
    packed = rows // 2
    count = 3 * blocks
    plane = grid[0] * grid[1] * grid[2]
    tall = devices // plane
    piece = vectors // plane
    me = lax.axis_index("nodes")
    level, place = me // plane, me % plane
    odd = me % 2
    partner = me + 1 - 2 * odd
    other = (me + devices - 1 + 2 * odd) % devices

    around = lambda shift, size: min(shift, size - shift)
    shifts = sorted(
        ((a, b, c) for a in range(grid[0]) for b in range(grid[1]) for c in range(grid[2]) if a + b + c > 0),
        key=lambda t: -(4 * around(t[0], grid[0]) + 4 * around(t[1], grid[1]) + t[2]),
    )
    at_a, at_b, at_c = place // (grid[1] * grid[2]), place // grid[2] % grid[1], place % grid[2]
    plane_peers = [
        ((at_a + a) % grid[0] * grid[1] + (at_b + b) % grid[1]) * grid[2] + (at_c + c) % grid[2]
        for a, b, c in shifts
    ]
    tall_peers = [
        (level + k) % tall * plane + place for k in sorted(range(1, tall), key=lambda k: -around(k, tall))
    ]

    loads = [
        pltpu.make_async_copy(src, dst, load_sem.at[i])
        for i, (src, dst) in enumerate(
            (
                (tan_ref.at[0], full.at[0]),
                (col_hbm, col_ref),
                (v_hbm, v_ref),
                (coup_ref, raw.at[pl.ds(0, blocks)]),
                (tan_ref.at[1], full.at[1]),
            )
        )
    ]
    loads[0].start()
    barrier = pltpu.get_barrier_semaphore()

    def greet(device):
        pl.semaphore_signal(barrier, inc=1, device_id=(device,), device_id_type=MESH)

    for peer in tall_peers:
        greet(peer)
    for peer in plane_peers:
        greet(level * plane + peer)
    greet(other)
    greet(partner)
    for load in loads[1:]:
        load.start()
    raw[blocks, 0] = jnp.zeros((size, size), jnp.bfloat16)
    low = lax.broadcasted_iota(jnp.int32, (half, vectors), 1) < lanes

    def turn(x):
        return pltpu.roll(x, lanes, axis=1)

    def pack(which, store):
        for b in range(blocks):
            top = full[which, pl.ds(b * size, half), :]
            bottom = full[which, pl.ds(b * size + half, half), :]
            store(0, b, jnp.where(low, top, turn(bottom)))
            store(1, b, jnp.where(low, turn(top), bottom))

    def unpack(which, group):
        for b in range(blocks):
            zero, one = group[0, pl.ds(b * half, half), :], group[1, pl.ds(b * half, half), :]
            full[which, pl.ds(b * size, half), :] = jnp.where(low, zero, turn(one))
            full[which, pl.ds(b * size + half, half), :] = jnp.where(low, turn(zero), one)

    def start_voltage(g, b, value):
        sv[g, pl.ds(b * half, half), :] = value
        own[0, g, pl.ds(b * half, half), :] = value.astype(jnp.bfloat16)

    def start_recovery(g, b, value):
        sw[g, pl.ds(b * half, half), :] = value

    loads[0].wait()
    pack(0, start_voltage)
    pl.semaphore_wait(barrier, 2 + (plane - 1) + (tall - 1))

    def send(step, g, b, side):
        span = pl.ds(b * half, half)
        dst, target = ((near, partner), (far, other))[side]
        return pltpu.make_async_remote_copy(
            src_ref=own.at[step, g, span, :],
            dst_ref=dst.at[step, g, span, :],
            send_sem=send_sem.at[step, g, side, b],
            recv_sem=recv_sem.at[step, g, side, b],
            device_id=(target,),
            device_id_type=MESH,
        )

    for g in range(GROUPS):
        for b in range(blocks):
            send(0, g, b, 1).start()
            send(0, g, b, 0).start()

    loads[1].wait()
    first = me * blocks
    names = [[(col_ref[r, k] - first + blocks * (devices + 1)) % (blocks * devices) for k in range(links)] for r in range(blocks)]
    loads[2].wait()
    volt = v_ref[...]
    factor = 1.0 + time_step * (1.0 - volt * volt)
    factor = jnp.concatenate([factor, factor], axis=0).T
    for s in range(STEPS):
        for b in range(blocks):
            top, bottom = (
                jnp.broadcast_to(factor[b * size + at : b * size + at + half, s : s + 1], (half, vectors))
                for at in (0, half)
            )
            coef[s, pl.ds(b * half, half), :] = jnp.where(low, top, bottom)
    loads[3].wait()
    starts = (blocks, 2 * blocks * (1 - odd), 2 * blocks * odd)
    for r in range(blocks):
        for c in range(count):
            at_r, at_k = blocks, 0
            for k in range(links):
                hit = names[r][k] == starts[c // blocks] + c % blocks
                at_r = jnp.where(hit, r, at_r)
                at_k = jnp.where(hit, k, at_k)
            block = raw[at_r, at_k]
            weights[pl.ds(r * size, half), pl.ds(c * size, size)] = block[:half]
            for side in range(2):
                weights[pl.ds(r * size + half, half), pl.ds(c * size + side * half, half)] = block[
                    half:, (1 - side) * half : (2 - side) * half
                ]

    def both(*values):
        return jnp.concatenate([y for x in values for y in (x, turn(x))], axis=0)

    def product(row_span, at, operand):
        return jnp.dot(
            weights[row_span, pl.ds(at * size, operand.shape[0])], operand, preferred_element_type=jnp.float32
        )

    def own_part(s, g):
        old_v, old_w = sv[g], sw[g]
        sv[g] = old_v * coef[s] - time_step * old_w
        sw[g] = old_w + time_step * recovery_rate * (old_v - recovery_damp * old_w)
        operand = both(*(own[s, g, pl.ds(b * half, half), :] for b in range(blocks)))
        acc[g] = product(pl.ds(0, rows), 0, operand)

    def near_part(s, g):
        for b in range(blocks):
            send(s, g, b, 0).wait_recv()
        operand = both(*(near[s, g, pl.ds(b * half, half), :] for b in range(blocks)))
        acc[g] += product(pl.ds(0, rows), blocks, operand)

    def finish(s, g):
        for b in range(blocks):
            send(s, g, b, 1).wait_recv()
        operand = both(*(far[s, g, pl.ds(b * half, half), :] for b in range(blocks)))
        for r in range(blocks):
            span = pl.ds(r * half, half)
            here = pl.ds(r * size, size)
            coupled = acc[g, here, :] + product(here, 2 * blocks, operand)
            new = sv[g, span, :] + time_step * jnp.where(low, coupled[:half], coupled[half:])
            sv[g, span, :] = new
            if s < STEPS - 1:
                own[s + 1, g, span, :] = new.astype(jnp.bfloat16)
                send(s + 1, g, r, 1).start()
                send(s + 1, g, r, 0).start()

    def gram_of(which):
        x = full[which]
        return lax.dot_general(
            x, x, (((0,), (0,)), ((), ())), precision=HIGH, preferred_element_type=jnp.float32
        )

    loads[4].wait()
    pack(1, start_recovery)
    for g in range(GROUPS):
        own_part(0, g)
    for s in range(STEPS):
        for g in range(GROUPS):
            near_part(s, g)
        for g in range(GROUPS):
            finish(s, g)
            if s < STEPS - 1:
                own_part(s + 1, g)
        if s == STEPS - 2:
            unpack(1, sw)
            store_w = pltpu.make_async_copy(full.at[1], state_ref.at[1], out_sem.at[1])
            store_w.start()
            gram_w = gram_of(1)
    unpack(0, sv)
    store_v = pltpu.make_async_copy(full.at[0], state_ref.at[0], out_sem.at[0])
    store_v.start()
    local = gram_w + gram_of(0)
    for i in range(plane):
        parts[i] = local[i * piece : (i + 1) * piece, :]

    def spread(phase, src, dst, target):
        return pltpu.make_async_remote_copy(
            src_ref=src,
            dst_ref=dst,
            send_sem=red_send.at[phase],
            recv_sem=red_recv.at[phase],
            device_id=(target,),
            device_id_type=MESH,
        )

    def all_of(phase, ref, slots):
        span = ref.at[pl.ds(0, slots)]
        return spread(phase, span, span, partner)

    for k, peer in enumerate(plane_peers):
        spread(0, parts.at[peer], got.at[k], level * plane + peer).start()

    all_of(0, got, plane - 1).wait_recv()
    mine = parts[place] + jnp.sum(got[...], axis=0)
    zbuf[level] = mine

    for peer in tall_peers:
        spread(1, zbuf.at[level], zbuf.at[level], peer).start()

    for s in range(STEPS):
        for g in range(GROUPS):
            for b in range(blocks):
                for side in range(2):
                    send(s, g, b, side).wait_send()
    all_of(0, got, plane - 1).wait_send()
    store_w.wait()
    store_v.wait()
    all_of(1, zbuf, tall - 1).wait_recv()
    total[place] = jnp.sum(zbuf[...], axis=0)

    for peer in plane_peers:
        spread(2, total.at[place], total.at[place], level * plane + peer).start()

    all_of(1, zbuf, tall - 1).wait_send()
    all_of(2, total, plane - 1).wait_recv()
    for i in range(plane):
        gram_ref[i * piece : (i + 1) * piece, :] = total[i]

    all_of(2, total, plane - 1).wait_send()


def factor_rows(gram, width, scratch):
    lane = lax.broadcasted_iota(jnp.int32, (8, width), 1)
    sub = lax.broadcasted_iota(jnp.int32, (8, width), 0)
    wide = lambda x: jnp.broadcast_to(x, (8, width))
    count = width // 8
    panels = [gram[8 * q : 8 * q + 8, :] for q in range(count)]
    upper, inverse = [], []
    for p in range(count):
        panel = panels[p]
        base = 8 * p
        cols = [wide(panel[:, base + k : base + k + 1]) for k in range(8)]
        for k in range(8):
            scratch[p, k] = cols[k]
        diag = {(s, k): wide(scratch[p, k, s : s + 1, :]) for k in range(8) for s in range(k, 8)}
        in_block = (lane >= base) & (lane < base + 8)
        mixed = jnp.where(in_block, jnp.where(lane - base == sub, 1.0, 0.0), panel)
        row_a = [wide(panel[s : s + 1, :]) for s in range(8)]
        row_c = [wide(mixed[s : s + 1, :]) for s in range(8)]
        nxt = [wide(panels[p + 1][:, base + k : base + k + 1]) for k in range(8)] if p + 1 < count else None
        nval = jnp.where(in_block, 0.0, panels[p + 1]) if p + 1 < count else None
        inv = []
        for i in range(8):
            inv.append(lax.rsqrt(diag[i, i]))
            row_a[i] = row_a[i] * inv[i]
            row_c[i] = row_c[i] * inv[i]
            if nxt: nxt[i] = nxt[i] * inv[i]
            for s in range(i + 1, 8):
                diag[s, i] = diag[s, i] * inv[i]
            for s in range(i + 1, 8):
                for k in range(i + 1, s + 1):
                    diag[s, k] = diag[s, k] - diag[s, i] * diag[k, i]
                row_a[s] = row_a[s] - diag[s, i] * row_a[i]
                row_c[s] = row_c[s] - diag[s, i] * row_c[i]
                if nxt: nxt[s] = nxt[s] - diag[s, i] * nxt[i]
            if nxt: nval = nval - nxt[i] * row_c[i]
        out_a, out_c = row_a[7], row_c[7]
        for s in range(7):
            out_a = jnp.where(sub == s, row_a[s], out_a)
            out_c = jnp.where(sub == s, row_c[s], out_c)
        upper.append(jnp.where(lane >= base + sub, out_a, 0.0))
        inverse.append(jnp.where(lane <= base + sub, out_c, 0.0))
        if nxt:
            panels[p + 1] = nval
        back = [None] * 8
        for i in range(7, -1, -1):
            value = row_c[i]
            for s in range(i + 1, 8):
                value = value - diag[s, i] * back[s]
            back[i] = value * inv[i]
        for q in range(p + 2, count):
            value = jnp.where(in_block, 0.0, panels[q])
            t = [wide(panels[q][:, base + k : base + k + 1]) * back[k] for k in range(8)]
            t = ((t[0] + t[1]) + (t[2] + t[3])) + ((t[4] + t[5]) + (t[6] + t[7]))
            panels[q] = value - t
    return upper, inverse


def basis_kernel(scale, gram_ref, state_ref, basis_ref, growth_ref, state, inverse, out, scratch, in_sem, out_sem):
    vectors = gram_ref.shape[0]
    load = pltpu.make_async_copy(state_ref, state, in_sem)
    load.start()
    upper, low = factor_rows(gram_ref[...], vectors, scratch)
    for p, (a, c) in enumerate(zip(upper, low)):
        growth_ref[8 * p : 8 * p + 8, :] = a * (1.0 / scale)
        inverse[8 * p : 8 * p + 8, :] = c * scale
    load.wait()
    copies = []
    for which in range(2):
        for at in range(0, state.shape[1], state.shape[1] // PIECES):
            span = pl.ds(at, state.shape[1] // PIECES)
            out[which, span, :] = lax.dot_general(
                state[which, span, :], inverse[...], (((1,), (1,)), ((), ())),
                precision=HIGH, preferred_element_type=jnp.float32,
            )
            copies.append(
                pltpu.make_async_copy(out.at[which, span, :], basis_ref.at[which, span, :], out_sem.at[len(copies)])
            )
            copies[-1].start()
    for copy in copies:
        copy.wait()


def local(tangent, base_v, coupling, columns, *, grid=(4, 4, 2)):
    blocks, links, size, _ = coupling.shape
    _, rows, vectors = tangent.shape
    devices = lax.axis_size("nodes")
    count = 3 * blocks
    plane = grid[0] * grid[1] * grid[2]
    tall, piece = devices // plane, vectors // plane
    vmem = pl.BlockSpec(memory_space=pltpu.VMEM)
    anywhere = pl.BlockSpec(memory_space=pl.ANY)
    f32, bf16 = jnp.float32, jnp.bfloat16
    dma = pltpu.SemaphoreType.DMA
    state, gram = pl.pallas_call(
        functools.partial(tangent_kernel, devices, grid),
        out_shape=(
            jax.ShapeDtypeStruct((2, rows, vectors), f32),
            jax.ShapeDtypeStruct((vectors, vectors), f32),
        ),
        in_specs=[pl.BlockSpec(memory_space=pltpu.HBM)] * 4,
        out_specs=(anywhere, vmem),
        scratch_shapes=[
            pltpu.VMEM((STEPS, rows), f32),
            pltpu.SMEM((blocks, links), jnp.int32),
            pltpu.VMEM((2, rows, vectors), f32),
            pltpu.VMEM((GROUPS, rows // 2, vectors), f32),
            pltpu.VMEM((GROUPS, rows // 2, vectors), f32),
            pltpu.VMEM((GROUPS, rows, vectors), f32),
            pltpu.VMEM((STEPS, rows // 2, vectors), f32),
            pltpu.VMEM((blocks + 1, links, size, size), bf16),
            pltpu.VMEM((rows, count * size), bf16),
            pltpu.VMEM((STEPS, GROUPS, rows // 2, vectors), bf16),
            pltpu.VMEM((STEPS, GROUPS, rows // 2, vectors), bf16),
            pltpu.VMEM((STEPS, GROUPS, rows // 2, vectors), bf16),
            pltpu.VMEM((plane, piece, vectors), f32),
            pltpu.VMEM((plane - 1, piece, vectors), f32),
            pltpu.VMEM((tall, piece, vectors), f32),
            pltpu.VMEM((plane, piece, vectors), f32),
            dma((5,)),
            dma((STEPS, GROUPS, 2, blocks)),
            dma((STEPS, GROUPS, 2, blocks)),
            dma((3,)),
            dma((3,)),
            dma((2,)),
        ],
        compiler_params=pltpu.CompilerParams(
            collective_id=0, has_side_effects=True, vmem_limit_bytes=40 * 2**20
        ),
    )(*(pltpu.with_memory_space_constraint(x, pltpu.HBM) for x in (tangent, base_v, coupling, columns)))
    scale = float((2.0 * rows * devices) ** 0.5)
    return pl.pallas_call(
        functools.partial(basis_kernel, scale),
        out_shape=(
            jax.ShapeDtypeStruct((2, rows, vectors), f32),
            jax.ShapeDtypeStruct((vectors, vectors), f32),
        ),
        in_specs=[vmem, anywhere],
        out_specs=(anywhere, vmem),
        scratch_shapes=[
            pltpu.VMEM((2, rows, vectors), f32),
            pltpu.VMEM((vectors, vectors), f32),
            pltpu.VMEM((2, rows, vectors), f32),
            pltpu.VMEM((vectors // 8, 8, 8, vectors), f32),
            dma,
            dma((2 * PIECES,)),
        ],
        compiler_params=pltpu.CompilerParams(vmem_limit_bytes=40 * 2**20),
    )(gram, state)


def solution(mesh):
    placed = (
        P(None, "nodes", None),
        P(None, "nodes"),
        P("nodes", None, None, None),
        P("nodes", None),
    )
    return jax.shard_map(
        local, mesh=mesh, in_specs=placed, out_specs=(P(None, "nodes", None), P()), check_vma=False
    )
```

```python
import functools

import jax
import jax.numpy as jnp
from jax import lax
from jax.experimental import pallas as pl
from jax.experimental.pallas import tpu as pltpu
from jax.sharding import PartitionSpec as P

STEPS = 4
GROUPS = 2
PIECES = 3
MESH = pl.DeviceIdType.MESH
HIGH = lax.Precision.HIGHEST

time_step = 0.1
recovery_rate = 0.08
recovery_damp = 0.8


def tangent_kernel(
    devices, grid, tan_ref, v_hbm, coup_ref, col_hbm, state_ref, gram_ref,
    v_ref, col_ref, full, sv, sw, acc, coef, raw, weights, own, near, far, parts, got, zbuf, total,
    load_sem, send_sem, recv_sem, red_send, red_recv, out_sem,
):
    blocks, links, size, _ = coup_ref.shape
    _, rows, vectors = full.shape
    half, lanes = size // 2, vectors // 2
    packed = rows // 2
    count = 3 * blocks
    plane = grid[0] * grid[1] * grid[2]
    tall = devices // plane
    piece = vectors // plane
    me = lax.axis_index("nodes")
    level, place = me // plane, me % plane
    odd = me % 2
    partner = me + 1 - 2 * odd
    other = (me + devices - 1 + 2 * odd) % devices

    around = lambda shift, size: min(shift, size - shift)
    shifts = sorted(
        ((a, b, c) for a in range(grid[0]) for b in range(grid[1]) for c in range(grid[2]) if a + b + c > 0),
        key=lambda t: -(4 * around(t[0], grid[0]) + 4 * around(t[1], grid[1]) + t[2]),
    )
    at_a, at_b, at_c = place // (grid[1] * grid[2]), place // grid[2] % grid[1], place % grid[2]
    plane_peers = [
        ((at_a + a) % grid[0] * grid[1] + (at_b + b) % grid[1]) * grid[2] + (at_c + c) % grid[2]
        for a, b, c in shifts
    ]
    tall_peers = [
        (level + k) % tall * plane + place for k in sorted(range(1, tall), key=lambda k: -around(k, tall))
    ]

    loads = [
        pltpu.make_async_copy(src, dst, load_sem.at[i])
        for i, (src, dst) in enumerate(
            (
                (tan_ref.at[0], full.at[0]),
                (col_hbm, col_ref),
                (v_hbm, v_ref),
                (coup_ref, raw.at[pl.ds(0, blocks)]),
                (tan_ref.at[1], full.at[1]),
            )
        )
    ]
    loads[0].start()
    barrier = pltpu.get_barrier_semaphore()

    def greet(device):
        pl.semaphore_signal(barrier, inc=1, device_id=(device,), device_id_type=MESH)

    for peer in tall_peers:
        greet(peer)
    for peer in plane_peers:
        greet(level * plane + peer)
    greet(other)
    greet(partner)
    for load in loads[1:]:
        load.start()
    raw[blocks, 0] = jnp.zeros((size, size), jnp.bfloat16)
    low = lax.broadcasted_iota(jnp.int32, (half, vectors), 1) < lanes

    def turn(x):
        return pltpu.roll(x, lanes, axis=1)

    def pack(which, store):
        for b in range(blocks):
            top = full[which, pl.ds(b * size, half), :]
            bottom = full[which, pl.ds(b * size + half, half), :]
            store(0, b, jnp.where(low, top, turn(bottom)))
            store(1, b, jnp.where(low, turn(top), bottom))

    def unpack(which, group):
        for b in range(blocks):
            zero, one = group[0, pl.ds(b * half, half), :], group[1, pl.ds(b * half, half), :]
            full[which, pl.ds(b * size, half), :] = jnp.where(low, zero, turn(one))
            full[which, pl.ds(b * size + half, half), :] = jnp.where(low, turn(zero), one)

    def start_voltage(g, b, value):
        sv[g, pl.ds(b * half, half), :] = value
        own[0, g, pl.ds(b * half, half), :] = value.astype(jnp.bfloat16)

    def start_recovery(g, b, value):
        sw[g, pl.ds(b * half, half), :] = value

    loads[0].wait()
    pack(0, start_voltage)
    pl.semaphore_wait(barrier, 2 + (plane - 1) + (tall - 1))

    def send(step, g, b, side):
        span = pl.ds(b * half, half)
        dst, target = ((near, partner), (far, other))[side]
        return pltpu.make_async_remote_copy(
            src_ref=own.at[step, g, span, :],
            dst_ref=dst.at[step, g, span, :],
            send_sem=send_sem.at[step, g, side, b],
            recv_sem=recv_sem.at[step, g, side, b],
            device_id=(target,),
            device_id_type=MESH,
        )

    for g in range(GROUPS):
        for b in range(blocks):
            send(0, g, b, 1).start()
            send(0, g, b, 0).start()

    loads[1].wait()
    first = me * blocks
    names = [[(col_ref[r, k] - first + blocks * (devices + 1)) % (blocks * devices) for k in range(links)] for r in range(blocks)]
    loads[2].wait()
    volt = v_ref[...]
    factor = 1.0 + time_step * (1.0 - volt * volt)
    factor = jnp.concatenate([factor, factor], axis=0).T
    for s in range(STEPS):
        for b in range(blocks):
            top, bottom = (
                jnp.broadcast_to(factor[b * size + at : b * size + at + half, s : s + 1], (half, vectors))
                for at in (0, half)
            )
            coef[s, pl.ds(b * half, half), :] = jnp.where(low, top, bottom)
    loads[3].wait()
    starts = (blocks, 2 * blocks * (1 - odd), 2 * blocks * odd)
    for r in range(blocks):
        for c in range(count):
            at_r, at_k = blocks, 0
            for k in range(links):
                hit = names[r][k] == starts[c // blocks] + c % blocks
                at_r = jnp.where(hit, r, at_r)
                at_k = jnp.where(hit, k, at_k)
            block = raw[at_r, at_k]
            weights[pl.ds(r * size, half), pl.ds(c * size, size)] = block[:half]
            for side in range(2):
                weights[pl.ds(r * size + half, half), pl.ds(c * size + side * half, half)] = block[
                    half:, (1 - side) * half : (2 - side) * half
                ]

    def both(*values):
        return jnp.concatenate([y for x in values for y in (x, turn(x))], axis=0)

    def product(row_span, at, operand):
        return jnp.dot(
            weights[row_span, pl.ds(at * size, operand.shape[0])], operand, preferred_element_type=jnp.float32
        )

    def own_part(s, g):
        old_v, old_w = sv[g], sw[g]
        sv[g] = old_v * coef[s] - time_step * old_w
        sw[g] = old_w + time_step * recovery_rate * (old_v - recovery_damp * old_w)
        operand = both(*(own[s, g, pl.ds(b * half, half), :] for b in range(blocks)))
        acc[g] = product(pl.ds(0, rows), 0, operand)

    def near_part(s, g):
        for b in range(blocks):
            send(s, g, b, 0).wait_recv()
        operand = both(*(near[s, g, pl.ds(b * half, half), :] for b in range(blocks)))
        acc[g] += product(pl.ds(0, rows), blocks, operand)

    def finish(s, g):
        operand = []
        for b in range(blocks):
            send(s, g, b, 1).wait_recv()
            operand.append(both(far[s, g, pl.ds(b * half, half), :]))
        operand = jnp.concatenate(operand, axis=0)
        for r in range(blocks):
            span = pl.ds(r * half, half)
            here = pl.ds(r * size, size)
            coupled = acc[g, here, :] + product(here, 2 * blocks, operand)
            new = sv[g, span, :] + time_step * jnp.where(low, coupled[:half], coupled[half:])
            sv[g, span, :] = new
            if s < STEPS - 1:
                own[s + 1, g, span, :] = new.astype(jnp.bfloat16)
                send(s + 1, g, r, 1).start()
                send(s + 1, g, r, 0).start()

    def gram_of(which):
        x = full[which]
        return lax.dot_general(
            x, x, (((0,), (0,)), ((), ())), precision=HIGH, preferred_element_type=jnp.float32
        )

    loads[4].wait()
    pack(1, start_recovery)
    for g in range(GROUPS):
        own_part(0, g)
    for s in range(STEPS):
        for g in range(GROUPS):
            near_part(s, g)
        for g in range(GROUPS):
            finish(s, g)
            if s < STEPS - 1:
                own_part(s + 1, g)
        if s == STEPS - 2:
            unpack(1, sw)
            store_w = pltpu.make_async_copy(full.at[1], state_ref.at[1], out_sem.at[1])
            store_w.start()
            gram_w = gram_of(1)
    unpack(0, sv)
    store_v = pltpu.make_async_copy(full.at[0], state_ref.at[0], out_sem.at[0])
    store_v.start()
    local = gram_w + gram_of(0)
    for i in range(plane):
        parts[i] = local[i * piece : (i + 1) * piece, :]

    def spread(phase, src, dst, target):
        return pltpu.make_async_remote_copy(
            src_ref=src,
            dst_ref=dst,
            send_sem=red_send.at[phase],
            recv_sem=red_recv.at[phase],
            device_id=(target,),
            device_id_type=MESH,
        )

    def all_of(phase, ref, slots):
        span = ref.at[pl.ds(0, slots)]
        return spread(phase, span, span, partner)

    for k, peer in enumerate(plane_peers):
        spread(0, parts.at[peer], got.at[k], level * plane + peer).start()

    all_of(0, got, plane - 1).wait_recv()
    mine = parts[place] + jnp.sum(got[...], axis=0)
    zbuf[level] = mine

    for peer in tall_peers:
        spread(1, zbuf.at[level], zbuf.at[level], peer).start()

    for s in range(STEPS):
        for g in range(GROUPS):
            for b in range(blocks):
                for side in range(2):
                    send(s, g, b, side).wait_send()
    all_of(0, got, plane - 1).wait_send()
    store_w.wait()
    store_v.wait()
    all_of(1, zbuf, tall - 1).wait_recv()
    total[place] = jnp.sum(zbuf[...], axis=0)

    for peer in plane_peers:
        spread(2, total.at[place], total.at[place], level * plane + peer).start()

    all_of(1, zbuf, tall - 1).wait_send()
    all_of(2, total, plane - 1).wait_recv()
    for i in range(plane):
        gram_ref[i * piece : (i + 1) * piece, :] = total[i]

    all_of(2, total, plane - 1).wait_send()


def factor_rows(gram, width, scratch):
    lane = lax.broadcasted_iota(jnp.int32, (8, width), 1)
    sub = lax.broadcasted_iota(jnp.int32, (8, width), 0)
    wide = lambda x: jnp.broadcast_to(x, (8, width))
    count = width // 8
    panels = [gram[8 * q : 8 * q + 8, :] for q in range(count)]
    upper, inverse = [], []
    for p in range(count):
        panel = panels[p]
        base = 8 * p
        cols = [wide(panel[:, base + k : base + k + 1]) for k in range(8)]
        for k in range(8):
            scratch[p, k] = cols[k]
        diag = {(s, k): wide(scratch[p, k, s : s + 1, :]) for k in range(8) for s in range(k, 8)}
        in_block = (lane >= base) & (lane < base + 8)
        mixed = jnp.where(in_block, jnp.where(lane - base == sub, 1.0, 0.0), panel)
        row_a = [wide(panel[s : s + 1, :]) for s in range(8)]
        row_c = [wide(mixed[s : s + 1, :]) for s in range(8)]
        nxt = [wide(panels[p + 1][:, base + k : base + k + 1]) for k in range(8)] if p + 1 < count else None
        nval = jnp.where(in_block, 0.0, panels[p + 1]) if p + 1 < count else None
        inv = []
        for i in range(8):
            inv.append(lax.rsqrt(diag[i, i]))
            row_a[i] = row_a[i] * inv[i]
            row_c[i] = row_c[i] * inv[i]
            if nxt: nxt[i] = nxt[i] * inv[i]
            for s in range(i + 1, 8):
                diag[s, i] = diag[s, i] * inv[i]
            for s in range(i + 1, 8):
                for k in range(i + 1, s + 1):
                    diag[s, k] = diag[s, k] - diag[s, i] * diag[k, i]
                row_a[s] = row_a[s] - diag[s, i] * row_a[i]
                row_c[s] = row_c[s] - diag[s, i] * row_c[i]
                if nxt: nxt[s] = nxt[s] - diag[s, i] * nxt[i]
            if nxt: nval = nval - nxt[i] * row_c[i]
        out_a, out_c = row_a[7], row_c[7]
        for s in range(7):
            out_a = jnp.where(sub == s, row_a[s], out_a)
            out_c = jnp.where(sub == s, row_c[s], out_c)
        upper.append(jnp.where(lane >= base + sub, out_a, 0.0))
        inverse.append(jnp.where(lane <= base + sub, out_c, 0.0))
        if nxt:
            panels[p + 1] = nval
        back = [None] * 8
        for i in range(7, -1, -1):
            value = row_c[i]
            for s in range(i + 1, 8):
                value = value - diag[s, i] * back[s]
            back[i] = value * inv[i]
        for q in range(p + 2, count):
            value = jnp.where(in_block, 0.0, panels[q])
            t = [wide(panels[q][:, base + k : base + k + 1]) * back[k] for k in range(8)]
            t = ((t[0] + t[1]) + (t[2] + t[3])) + ((t[4] + t[5]) + (t[6] + t[7]))
            panels[q] = value - t
    return upper, inverse


def basis_kernel(scale, gram_ref, state_ref, basis_ref, growth_ref, state, inverse, out, growth, scratch, in_sem, out_sem):
    vectors = gram_ref.shape[0]
    load = pltpu.make_async_copy(state_ref, state, in_sem)
    load.start()
    upper, low = factor_rows(gram_ref[...], vectors, scratch)
    for p, (a, c) in enumerate(zip(upper, low)):
        growth[8 * p : 8 * p + 8, :] = a * (1.0 / scale)
        inverse[8 * p : 8 * p + 8, :] = c * scale
    load.wait()
    copies = [pltpu.make_async_copy(growth, growth_ref, out_sem.at[2 * PIECES])]
    copies[0].start()
    for which in range(2):
        for at in range(0, state.shape[1], state.shape[1] // PIECES):
            span = pl.ds(at, state.shape[1] // PIECES)
            out[which, span, :] = lax.dot_general(
                state[which, span, :], inverse[...], (((1,), (1,)), ((), ())),
                precision=HIGH, preferred_element_type=jnp.float32,
            )
            copies.append(
                pltpu.make_async_copy(out.at[which, span, :], basis_ref.at[which, span, :], out_sem.at[len(copies) - 1])
            )
            copies[-1].start()
    for copy in copies:
        copy.wait()


def local(tangent, base_v, coupling, columns, *, grid=(4, 4, 2)):
    blocks, links, size, _ = coupling.shape
    _, rows, vectors = tangent.shape
    devices = lax.axis_size("nodes")
    count = 3 * blocks
    plane = grid[0] * grid[1] * grid[2]
    tall, piece = devices // plane, vectors // plane
    vmem = pl.BlockSpec(memory_space=pltpu.VMEM)
    anywhere = pl.BlockSpec(memory_space=pl.ANY)
    f32, bf16 = jnp.float32, jnp.bfloat16
    dma = pltpu.SemaphoreType.DMA
    state, gram = pl.pallas_call(
        functools.partial(tangent_kernel, devices, grid),
        out_shape=(
            jax.ShapeDtypeStruct((2, rows, vectors), f32),
            jax.ShapeDtypeStruct((vectors, vectors), f32),
        ),
        in_specs=[pl.BlockSpec(memory_space=pltpu.HBM)] * 4,
        out_specs=(anywhere, vmem),
        scratch_shapes=[
            pltpu.VMEM((STEPS, rows), f32),
            pltpu.SMEM((blocks, links), jnp.int32),
            pltpu.VMEM((2, rows, vectors), f32),
            pltpu.VMEM((GROUPS, rows // 2, vectors), f32),
            pltpu.VMEM((GROUPS, rows // 2, vectors), f32),
            pltpu.VMEM((GROUPS, rows, vectors), f32),
            pltpu.VMEM((STEPS, rows // 2, vectors), f32),
            pltpu.VMEM((blocks + 1, links, size, size), bf16),
            pltpu.VMEM((rows, count * size), bf16),
            pltpu.VMEM((STEPS, GROUPS, rows // 2, vectors), bf16),
            pltpu.VMEM((STEPS, GROUPS, rows // 2, vectors), bf16),
            pltpu.VMEM((STEPS, GROUPS, rows // 2, vectors), bf16),
            pltpu.VMEM((plane, piece, vectors), f32),
            pltpu.VMEM((plane - 1, piece, vectors), f32),
            pltpu.VMEM((tall, piece, vectors), f32),
            pltpu.VMEM((plane, piece, vectors), f32),
            dma((5,)),
            dma((STEPS, GROUPS, 2, blocks)),
            dma((STEPS, GROUPS, 2, blocks)),
            dma((3,)),
            dma((3,)),
            dma((2,)),
        ],
        compiler_params=pltpu.CompilerParams(
            collective_id=0, has_side_effects=True, vmem_limit_bytes=40 * 2**20
        ),
    )(*(pltpu.with_memory_space_constraint(x, pltpu.HBM) for x in (tangent, base_v, coupling, columns)))
    scale = float((2.0 * rows * devices) ** 0.5)
    return pl.pallas_call(
        functools.partial(basis_kernel, scale),
        out_shape=(
            jax.ShapeDtypeStruct((2, rows, vectors), f32),
            jax.ShapeDtypeStruct((vectors, vectors), f32),
        ),
        in_specs=[vmem, anywhere],
        out_specs=(anywhere, anywhere),
        scratch_shapes=[
            pltpu.VMEM((2, rows, vectors), f32),
            pltpu.VMEM((vectors, vectors), f32),
            pltpu.VMEM((2, rows, vectors), f32),
            pltpu.VMEM((vectors, vectors), f32),
            pltpu.VMEM((vectors // 8, 8, 8, vectors), f32),
            dma,
            dma((2 * PIECES + 1,)),
        ],
        compiler_params=pltpu.CompilerParams(vmem_limit_bytes=40 * 2**20),
    )(gram, state)


def solution(mesh):
    placed = (
        P(None, "nodes", None),
        P(None, "nodes"),
        P("nodes", None, None, None),
        P("nodes", None),
    )
    return jax.shard_map(
        local, mesh=mesh, in_specs=placed, out_specs=(P(None, "nodes", None), P()), check_vma=False
    )
```
